32 devices in a mesh: fluid: 4 (over z), sub: 4 (over y, x), struct: 2 (over core).
Axes of the slice: x: 2, y: 2, z: 4, core: 2. Of those that a mesh axis runs over, the one named last changes fastest.
Arguments:
- velocity: float32 [16, 64, 3, 256], P('fluid', 'sub'), may hold values from -6 to 6
- pressure: float32 [16, 64, 256], P('fluid', 'sub'), may hold values from -6 to 6
- viscosity: float32 [16, 64, 256], P('fluid', 'sub'), may hold values from 0.02 to 0.15
- marker_force: float32 [2048, 3, 128], P(('fluid', 'sub', 'struct')), may hold values from -24 to 24
- marker_offset: float32 [2048, 3, 128], P(('fluid', 'sub', 'struct')), may hold values from 0 to 1
- cell_base: int32 [2048, 3, 128], P(('fluid', 'sub', 'struct')), may hold values from 0 to 253, as said below
- block_slab: int32 [2048, 1], P(('fluid', 'sub', 'struct')), may hold values from 0 to 3; in each aligned block of 64 rows (0 to 63, 64 to 127, ...) at most 32 rows name the same one
Outputs:
- new_velocity: float32 [16, 64, 3, 256], P('fluid', 'sub')
- marker_velocity: float32 [2048, 3, 128], P(('fluid', 'sub', 'struct'))
The draws below stay inside these ranges and needn't reach their ends.
Inputs may be any that keep to these rules, and one draw needn't show every extreme that they name: cell_base[b,0,m] lies in 0 to 3, cell_base[b,1,m] in 0 to 15 and cell_base[b,2,m] in 1 to 253. `block_slab`: within the 64 blocks of one device no slab is named more than 32 times.
All inputs are finite; a program needn't handle non-finite values.
Results may differ from the reference program's by a relative error of at most 0.0034.
Values may be sent and summed in bfloat16 or wider, within the bound.
A program may use at most 64 MiB of HBM per device.

```python
import math
import jax
import jax.numpy as jnp
import numpy as np
from jax import lax

CX = 4
CY = 16
NZ = 256
M = 128
MB = 64
SLABS = 4
SUBS = 4
PAIR_BLOCKS = 128
CAP = 32
NX = 16
NY = 64
NBLK = 2048


def draw_cell_base(key, part):
    keys = jax.random.split(jax.random.fold_in(key, 7), 3)
    first = jax.random.randint(keys[0], (NBLK, 1, M), 0, CX, dtype=jnp.int32)
    second = jax.random.randint(keys[1], (NBLK, 1, M), 0, CY, dtype=jnp.int32)
    third = jax.random.randint(keys[2], (NBLK, 1, M), 1, NZ - 2, dtype=jnp.int32)
    first = first.at[0, 0, 0].set(0).at[0, 0, 1].set(CX - 1)
    second = second.at[0, 0, 1].set(CY - 1)
    third = third.at[0, 0, 0].set(NZ - 3)
    return jnp.concatenate([first, second, third], axis=1)


def block_levels(own_key, dims, cuts, low, top_value):
    loudness, own = 1.0, jax.random.fold_in(own_key, 6)
    for dim, blocks in cuts:
        heights = jnp.exp(jax.random.uniform(jax.random.fold_in(own, dim), (blocks,), jnp.float32, low / len(cuts), top_value / len(cuts)))
        loudness = loudness * jnp.repeat(heights, dims[dim] // blocks).reshape([-1 if axis == dim else 1 for axis in range(len(dims))])
    return loudness


def deal_out(stream_key, own, number, rows, number_of, top, most, skew):
    ranking = jax.random.permutation(stream_key, number_of)
    crowded, usual = shares(number_of, rows * top, most, skew, True), shares(number_of, rows * top, most, skew, False)
    places = jnp.arange(number_of)

    def named(lengths, rotation):
        used = int((lengths > 0).sum())
        fixed = max(1, used // 4)
        shifted = fixed + (places - fixed + rotation * (used - fixed)) % max(1, number_of - fixed)
        return jnp.zeros((number_of,), jnp.int32).at[ranking[jnp.where(places < fixed, places, shifted)]].set(jnp.asarray(lengths, jnp.int32))

    lengths = jnp.where(number % 4 == 0, named(crowded, number // 4), named(usual, number - number // 4 - 1))
    mixed = jax.random.permutation(jax.random.fold_in(own, 3), number_of)
    donor, sink = mixed[0:number_of // 2 * 2:2], mixed[1:number_of // 2 * 2:2]
    slack = jnp.minimum(lengths[donor] - 1, most - lengths[sink]) // 2
    slack = jnp.where((donor == ranking[0]) | (sink == ranking[0]) | (lengths[sink] == 0), 0, jnp.maximum(slack, 0))
    shifted = jax.random.randint(jax.random.fold_in(own, 4), (number_of // 2,), 0, 1 << 20) % (slack + 1)
    lengths = lengths.at[donor].add(-shifted).at[sink].add(shifted)
    labels = jnp.searchsorted(jnp.cumsum(lengths), jnp.arange(rows * top), side="right").astype(jnp.int32)
    grid = labels.reshape(top, rows).T
    grid = grid[jax.random.permutation(jax.random.fold_in(own, 1), rows)]
    rotation = jax.random.randint(jax.random.fold_in(own, 2), (rows, 1), 0, top)
    return jnp.take_along_axis(grid, (jnp.arange(top)[None, :] + rotation) % top, axis=1)


def shares(count, total, most, lean, full):
    loads = [(1 << 20) // math.isqrt(rank ** lean) + 1 for rank in range(1, count + 1)]
    largest = most if full else min(most, max(-(-total // count), total * loads[0] // sum(loads)))
    least = 1 if total - largest >= count - 1 else 0
    holding, surplus = [largest] + [least] * (count - 1), total - largest - least * (count - 1)
    while surplus > 0:
        candidates = [i for i in range(1, count) if holding[i] < largest] or [i for i in range(1, count) if holding[i] < most]
        pool, remaining = sum([loads[i] for i in candidates]), surplus
        for i in candidates:
            addition = min(most - holding[i], max(1, remaining * loads[i] // pool), surplus)
            holding[i] = holding[i] + addition
            surplus = surplus - addition
    return np.array(holding)


def scatter_about(key, dims, scale, most, cuts=(), kind=jnp.bfloat16):
    loudness = block_levels(key, dims, cuts, -0.22, 0.18) if cuts else 1.0
    values = jax.random.normal(key, dims, jnp.float32) * scale * loudness
    return jnp.minimum(jnp.maximum(values, -most), most).astype(kind)


def setup_inputs(seed: int = 0) -> dict:
    splits = jax.random.split(jax.random.key(seed), 8)
    velocity = scatter_about(splits[0], (NX, NY, 3, NZ), 1.0, 6.0, ((0, 4), (1, 4)), jnp.float32)
    pressure = scatter_about(splits[1], (NX, NY, NZ), 1.0, 6.0, ((0, 4), (1, 4)), jnp.float32)
    viscosity = jnp.clip(jnp.exp(math.log(0.15) - 2.014903 * jax.random.uniform(splits[2], (NX, NY, NZ), jnp.float32) ** block_levels(splits[2], (NX, NY, NZ), ((0, 4), (1, 4)), -0.2, 0.2)), 0.02, 0.15)
    marker_force = scatter_about(splits[3], (NBLK, 3, M), 4.0, 24.0, ((0, 32),), jnp.float32)
    marker_offset = jnp.clip(1.0 * jax.random.uniform(splits[4], (NBLK, 3, M), jnp.float32) ** block_levels(splits[4], (NBLK, 3, M), ((0, 32),), -0.2, 0.2), 0.0, 1.0)
    cell_base = draw_cell_base(jax.random.fold_in(splits[7], 71), 0)
    block_slab_keys = jax.random.split(jax.random.fold_in(splits[6], 1), NBLK // MB)
    block_slab_turns = jax.random.permutation(jax.random.fold_in(splits[6], 3), NBLK // MB)
    block_slab = jax.vmap(lambda own, number: deal_out(jax.random.fold_in(splits[6], 2), own, number, MB, SLABS, 1, CAP, 2))(block_slab_keys, block_slab_turns).reshape((NBLK, 1))
    return dict(velocity=velocity, pressure=pressure, viscosity=viscosity, marker_force=marker_force, marker_offset=marker_offset, cell_base=cell_base, block_slab=block_slab)


neighbour_steps = ((1, 0, 0), (-1, 0, 0), (0, 1, 0), (0, -1, 0), (0, 0, 1), (0, 0, -1))

def kernel_weight(distance):
    inside = jnp.minimum(distance, 1.0)
    beyond = jnp.clip(distance - 1.0, 0.0, 1.0)
    inner = (3.0 - 2.0 * inside + jnp.sqrt(1.0 + 4.0 * inside - 4.0 * inside * inside)) * 0.125
    outer = (3.0 - 2.0 * beyond - jnp.sqrt(1.0 + 4.0 * beyond - 4.0 * beyond * beyond)) * 0.125
    return jnp.where(distance < 1.0, inner, outer)

def offset(array, first, second, third):
    extent_first = array.shape[0] - 2
    extent_second = array.shape[1] - 2
    extent_third = array.shape[-1] - 2
    return array[1 + first:1 + first + extent_first, 1 + second:1 + second + extent_second, ..., 1 + third:1 + third + extent_third]

def momentum(old_pad, force):
    velocity_pad = old_pad[:, :, 0:3]
    pressure_pad = old_pad[:, :, 3]
    viscosity_pad = old_pad[:, :, 4]
    centre = offset(velocity_pad, 0, 0, 0)
    viscosity_centre = offset(viscosity_pad, 0, 0, 0)[:, :, None]
    pressure_centre = offset(pressure_pad, 0, 0, 0)
    viscous = jnp.zeros_like(centre)
    for neighbour in neighbour_steps:
        neighbour_value = offset(velocity_pad, neighbour[0], neighbour[1], neighbour[2])
        face_viscosity = 0.5 * (viscosity_centre + offset(viscosity_pad, neighbour[0], neighbour[1], neighbour[2])[:, :, None])
        viscous = viscous + face_viscosity * (neighbour_value - centre)
    gradient = jnp.stack([offset(pressure_pad, 1, 0, 0) - pressure_centre, offset(pressure_pad, 0, 1, 0) - pressure_centre, offset(pressure_pad, 0, 0, 1) - pressure_centre], axis=2)
    return centre + 0.5 * (viscous - gradient + force)

def through_bfloat(values):
    return lax.optimization_barrier(values.astype(jnp.bfloat16)).astype(jnp.float32)

def reference(velocity, pressure, viscosity, marker_force, marker_offset, cell_base, block_slab):
    total_blocks = marker_force.shape[0]
    block_index = jnp.arange(total_blocks, dtype=jnp.int32)
    owner_sub = block_index // PAIR_BLOCKS % SUBS
    slab_index = block_slab[:, 0]
    global_x = (slab_index * CX)[:, None] + cell_base[:, 0, :]
    global_y = (owner_sub * CY)[:, None] + cell_base[:, 1, :]
    global_z = cell_base[:, 2, :]
    reaches = (-1.0, 0.0, 1.0, 2.0)
    weight_x = [kernel_weight(jnp.abs(reach - marker_offset[:, 0, :])) for reach in reaches]
    weight_y = [kernel_weight(jnp.abs(reach - marker_offset[:, 1, :])) for reach in reaches]
    weight_z = [kernel_weight(jnp.abs(reach - marker_offset[:, 2, :])) for reach in reaches]
    component = jnp.arange(3, dtype=jnp.int32)[None, :, None]
    spread_pad = jnp.zeros((NX + 3, NY + 3, 3, NZ), jnp.float32)
    for index_x in range(4):
        row_x = (global_x + index_x)[:, None, :]
        for index_y in range(4):
            row_y = (global_y + index_y)[:, None, :]
            plane = through_bfloat(weight_x[index_x] * weight_y[index_y])[:, None, :]
            for index_z in range(4):
                depth_cell = (global_z + index_z - 1)[:, None, :]
                loaded = through_bfloat(marker_force * weight_z[index_z][:, None, :])
                spread_pad = spread_pad.at[row_x, row_y, component, depth_cell].add(plane * loaded)
    spread = spread_pad[1:NX + 1, 1:NY + 1]
    stacked = jnp.concatenate([velocity, pressure[:, :, None], viscosity[:, :, None]], axis=2)
    old_pad = jnp.pad(stacked, ((1, 1), (1, 1), (0, 0), (1, 1)))
    fresh = momentum(old_pad, spread)
    rounded = through_bfloat(fresh)
    field_pad = jnp.pad(rounded, ((1, 2), (1, 2), (0, 0), (0, 0)))
    sampled = jnp.zeros(marker_force.shape, jnp.float32)
    for index_x in range(4):
        row_x = (global_x + index_x)[:, None, :]
        for index_y in range(4):
            row_y = (global_y + index_y)[:, None, :]
            plane = (weight_x[index_x] * weight_y[index_y])[:, None, :]
            for index_z in range(4):
                depth_cell = (global_z + index_z - 1)[:, None, :]
                depth_weight = through_bfloat(weight_z[index_z])[:, None, :]
                values = field_pad[row_x, row_y, component, depth_cell]
                sampled = sampled + plane * (values * depth_weight)
    return (fresh, sampled)
```

```python
import functools

import jax
import jax.numpy as jnp
from jax import lax
from jax.experimental import pallas as pl
from jax.experimental.pallas import tpu as pltpu
from jax.sharding import PartitionSpec as P

MESH = pl.DeviceIdType.MESH
RIM = 8
REACH = 3
MIB = 1 << 20


def stencil(offsets):
    root = jnp.sqrt(1.0 + 4.0 * offsets - 4.0 * offsets * offsets)
    low = 3.0 - 2.0 * offsets
    high = 1.0 + 2.0 * offsets
    return (
        (low - root) * 0.125,
        (low + root) * 0.125,
        (high + root) * 0.125,
        (high - root) * 0.125,
    )


def place(weights, dim, shift):
    result = jnp.zeros(shift.shape, jnp.float32)
    for n in range(4):
        result = jnp.where(shift == n - 1, weights[n][dim : dim + 1, :], result)
    return result


def spread_kernel(ex, ey, slab_ref, force_ref, offset_ref, base_ref, out_ref, acc):
    blocks, _, markers = force_ref.shape
    depth = acc.shape[3]
    rows = ey + RIM
    span = ex + REACH
    acc[...] = jnp.zeros_like(acc)
    xs = lax.broadcasted_iota(jnp.int32, (span, markers), 0) - 1
    ys = lax.broadcasted_iota(jnp.int32, (rows, markers), 0)
    ys = jnp.where(ys == ey + 2, -1, jnp.where(ys > ey + 2, -100, ys))
    zs = lax.broadcasted_iota(jnp.int32, (depth, markers), 0)

    def step(b, carry):
        start = slab_ref[b] * ex
        base = base_ref[b]
        force = force_ref[b]
        weights = stencil(offset_ref[b])
        wx = place(weights, 0, xs - base[0:1])
        wy = place(weights, 1, ys - base[1:2])
        wz = place(weights, 2, zs - base[2:3])
        plane = jnp.concatenate([wx[i : i + 1] * wy for i in range(span)], axis=0)
        plane = plane.astype(jnp.bfloat16)
        for c in range(3):
            loaded = (wz * force[c : c + 1]).astype(jnp.bfloat16)
            term = lax.dot_general(
                plane, loaded, (((1,), (1,)), ((), ())), preferred_element_type=jnp.float32
            )
            acc[pl.ds(start, span), c] += term.reshape(span, rows, depth)
        return carry

    lax.fori_loop(0, blocks, step, 0, unroll=2)

    def pack(x, carry):
        for c in range(3):
            out_ref[x, c] = acc[x + 1, c, 0:ey, :].astype(jnp.bfloat16)
        parts = [acc[x + 1, c, ey : ey + 3, :] for c in range(3)]
        parts.append(jnp.zeros((ey - 9, depth), jnp.float32))
        out_ref[x, 3] = jnp.concatenate(parts, axis=0).astype(jnp.bfloat16)
        return carry

    lax.fori_loop(0, out_ref.shape[0], pack, 0)


def sample_kernel(ex, ey, slab_ref, offset_ref, base_ref, field_ref, out_ref):
    blocks, _, markers = offset_ref.shape
    depth = field_ref.shape[3]
    span = ex + REACH
    xs = lax.broadcasted_iota(jnp.int32, (span, markers), 0) - 1
    ys = lax.broadcasted_iota(jnp.int32, (ey, markers), 0)
    rim = lax.broadcasted_iota(jnp.int32, (ey, markers), 0)
    turn = rim % 3
    rim = jnp.where(rim >= 9, -100, jnp.where(turn == 2, -1, ey + turn))
    zs = lax.broadcasted_iota(jnp.int32, (depth, markers), 0)

    def step(b, carry):
        start = slab_ref[b] * ex
        base = base_ref[b]
        weights = stencil(offset_ref[b])
        wx = place(weights, 0, xs - base[0:1])
        wy = place(weights, 1, ys - base[1:2])
        wr = place(weights, 1, rim - base[1:2])
        wz = place(weights, 2, zs - base[2:3]).astype(jnp.bfloat16)
        cells = field_ref[pl.ds(start, span)].reshape(span * 4 * ey, depth)
        sums = jnp.dot(cells, wz, preferred_element_type=jnp.float32)
        sums = sums.reshape(span, 4 * ey, markers)
        across = sums[0] * wx[0:1]
        for i in range(1, span):
            across = across + sums[i] * wx[i : i + 1]
        edge = across[3 * ey : 4 * ey] * wr
        found = []
        for c in range(3):
            own = jnp.sum(across[c * ey : (c + 1) * ey] * wy, axis=0, keepdims=True)
            found.append(own + jnp.sum(edge[3 * c : 3 * c + 3], axis=0, keepdims=True))
        out_ref[b] = jnp.concatenate(found, axis=0)
        return carry

    lax.fori_loop(0, blocks, step, 0, unroll=2)


def grid_kernel(
    slabs, subs,
    old_ref, part_ref, fresh_ref, field_ref,
    pair, outgoing, incoming, total, rims, xhalo, yhalo, my_rim, near_rim,
    sem_pair, sem_slab, sem_total, sem_rim, sem_x, sem_y, sem_near,
    sem_field, sem_edge, sem_forward,
):
    f, s, t = lax.axis_index("fluid"), lax.axis_index("sub"), lax.axis_index("struct")
    ex, _, ey, depth = old_ref.shape
    hx = ex // 2
    other = (f, s, 1 - t)
    has_low, has_high = s > 0, s < subs - 1
    has_left, has_right = f > 0, f < slabs - 1

    def copy(src, dst, sems, index, device):
        return pltpu.make_async_remote_copy(
            src_ref=src,
            dst_ref=dst,
            send_sem=sems.at[(0,) + index],
            recv_sem=sems.at[(1,) + index],
            device_id=device,
            device_id_type=MESH,
        )

    barrier = pltpu.get_barrier_semaphore()

    def greet(device):
        pl.semaphore_signal(barrier, inc=1, device_id=device, device_id_type=MESH)

    greet(other)

    def greet_slab(d, carry):
        greet((lax.rem(f + d, slabs), s, t))
        return carry

    lax.fori_loop(1, slabs, greet_slab, 0)
    for present, step in ((has_low, -1), (has_high, 1)):

        @pl.when(present)
        def _(step=step):
            greet((f, s + step, t))
            greet((f, s + step, 1 - t))

    beside = has_low.astype(jnp.int32) + has_high.astype(jnp.int32)
    pl.semaphore_wait(barrier, slabs + 2 * beside)

    def pair_copy(slab):
        return copy(part_ref.at[slab, 1 - t], pair.at[slab], sem_pair, (slab,), other)

    def start_pair(d, carry):
        pair_copy(lax.rem(f + d, slabs)).start()
        return carry

    lax.fori_loop(1, slabs + 1, start_pair, 0)

    x_copies = (
        (has_left, has_right, copy(old_ref.at[0], xhalo.at[1], sem_x, (1,), (f - 1, s, t)), 1),
        (has_right, has_left, copy(old_ref.at[ex - 1], xhalo.at[0], sem_x, (0,), (f + 1, s, t)), 0),
    )
    y_copies = (
        (has_low, has_high,
         copy(old_ref.at[:, :, 0:8], yhalo.at[1], sem_y, (1,), (f, s - 1, t)), 1),
        (has_high, has_low,
         copy(old_ref.at[:, :, ey - 8 : ey], yhalo.at[0], sem_y, (0,), (f, s + 1, t)), 0),
    )
    for copies, halo in ((x_copies, xhalo), (y_copies, yhalo)):
        for sends, receives, item, slot in copies:
            pl.when(sends)(item.start)

            @pl.when(jnp.logical_not(receives))
            def _(halo=halo, slot=slot):
                halo[slot] = jnp.zeros(halo.shape[1:], halo.dtype)

    def slab_copy(d):
        return copy(
            outgoing.at[d], incoming.at[d], sem_slab, (d,), (lax.rem(f + d, slabs), s, t)
        )

    def send_slab(d, carry):
        slab = lax.rem(f + d, slabs)
        pair_copy(slab).wait_recv()
        both = part_ref[slab, t].astype(jnp.float32) + pair[slab].astype(jnp.float32)
        outgoing[d] = both.astype(jnp.bfloat16)
        slab_copy(d).start()
        return carry

    lax.fori_loop(1, slabs, send_slab, 0)
    pair_copy(f).wait_recv()
    total[t] = part_ref[f, t].astype(jnp.float32) + pair[f].astype(jnp.float32)

    def add_slab(d, carry):
        slab_copy(d).wait_recv()
        total[t] += incoming[d].astype(jnp.float32)
        return carry

    lax.fori_loop(1, slabs, add_slab, 0)

    total_copy = copy(total.at[t], total.at[t], sem_total, (t,), other)
    total_back = copy(total.at[1 - t], total.at[1 - t], sem_total, (1 - t,), other)
    total_copy.start()
    for sends, receives, step, slot in ((has_high, has_low, 1, 0), (has_low, has_high, -1, 1)):

        @pl.when(sends)
        def _(step=step, slot=slot):
            for core in range(2):
                to = lax.rem(t + core, 2)
                pltpu.make_async_remote_copy(
                    src_ref=total.at[t, :, 3],
                    dst_ref=rims.at[slot, t],
                    send_sem=sem_rim.at[0, slot, core],
                    recv_sem=sem_rim.at[1, slot, t],
                    device_id=(f, s + step, to),
                    device_id_type=MESH,
                ).start()

        @pl.when(jnp.logical_not(receives))
        def _(slot=slot):
            rims[slot] = jnp.zeros(rims.shape[1:], rims.dtype)

    for copies in (x_copies, y_copies):
        for _, receives, item, _ in copies:
            pl.when(receives)(item.wait_recv)
    total_back.wait_recv()
    for receives, slot in ((has_low, 0), (has_high, 1)):

        @pl.when(receives)
        def _(slot=slot):
            for core in range(2):
                pltpu.make_async_remote_copy(
                    src_ref=total.at[t, :, 3],
                    dst_ref=rims.at[slot, core],
                    send_sem=sem_rim.at[0, slot, core],
                    recv_sem=sem_rim.at[1, slot, core],
                    device_id=other,
                    device_id_type=MESH,
                ).wait_recv()

    row = lax.broadcasted_iota(jnp.int32, (ey, depth), 0)
    lane = lax.broadcasted_iota(jnp.int32, (ey, depth), 1)
    here = 1 + ex * f

    def around(x, i):
        mid = old_ref[x, i]
        return (
            mid,
            old_ref[x + 1, i] if x < ex - 1 else xhalo[1, i],
            old_ref[x - 1, i] if x > 0 else xhalo[0, i],
            jnp.where(row == ey - 1, yhalo[1, x, i, 0:1, :], pltpu.roll(mid, ey - 1, 0)),
            jnp.where(row == 0, yhalo[0, x, i, 7:8, :], pltpu.roll(mid, 1, 0)),
            jnp.where(lane == depth - 1, 0.0, pltpu.roll(mid, depth - 1, 1)),
            jnp.where(lane == 0, 0.0, pltpu.roll(mid, 1, 1)),
        )

    for x in range(ex):
        pressure = around(x, 3)
        viscosity = around(x, 4)
        faces = [0.5 * (viscosity[0] + beside) for beside in viscosity[1:]]
        half, xi = x // hx, x % hx
        edge_rows = []
        for c in range(3):
            old = around(x, c)
            viscous = jnp.zeros((ey, depth), jnp.float32)
            for n in range(6):
                viscous = viscous + faces[n] * (old[n + 1] - old[0])
            slope = pressure[1 + 2 * c] - pressure[0]
            force = total[half, xi, c]
            low0 = rims[0, half, xi, 3 * c : 3 * c + 1, :]
            low1 = rims[0, half, xi, 3 * c + 1 : 3 * c + 2, :]
            top = rims[1, half, xi, 3 * c + 2 : 3 * c + 3, :]
            force = force + jnp.where(
                row == 0, low0, jnp.where(row == 1, low1, jnp.where(row == ey - 1, top, 0.0))
            )
            new = old[0] + 0.5 * (viscous - slope + force)
            fresh_ref[x, c] = new
            field_ref[here + x, c] = new.astype(jnp.bfloat16)
            edge_rows += [new[0:2], new[ey - 1 : ey]]
        edge_rows.append(jnp.zeros((ey - 9, depth), jnp.float32))
        my_rim[x] = jnp.concatenate(edge_rows, axis=0).astype(jnp.bfloat16)

    near_copies = (
        (has_high, has_low, copy(my_rim, near_rim.at[0], sem_near, (0,), (f, s + 1, t)), 0),
        (has_low, has_high, copy(my_rim, near_rim.at[1], sem_near, (1,), (f, s - 1, t)), 1),
    )
    for sends, receives, item, slot in near_copies:
        pl.when(sends)(item.start)

        @pl.when(jnp.logical_not(receives))
        def _(slot=slot):
            near_rim[slot] = jnp.zeros(near_rim.shape[1:], near_rim.dtype)

    def field_copy(slab, d, to):
        part = field_ref.at[pl.ds(1 + ex * slab + hx * t, hx), 0:3]
        return copy(part, part, sem_field, (d,), (to, s, t))

    def edge_copy(slab, d, to):
        part = field_ref.at[pl.ds(1 + ex * slab + hx * t, hx), 3]
        return copy(part, part, sem_edge, (d,), (to, s, t))

    def forward_copy(slab, d, core):
        part = field_ref.at[pl.ds(1 + ex * slab + hx * core, hx)]
        return copy(part, part, sem_forward, (d,), other)

    def start_field(d, carry):
        field_copy(f, d, lax.rem(f + d, slabs)).start()
        return carry

    lax.fori_loop(1, slabs, start_field, 0)
    for outside in (0, slabs * ex + 1, slabs * ex + 2):
        field_ref[outside] = jnp.zeros(field_ref.shape[1:], field_ref.dtype)
    for sends, receives, item, slot in near_copies:
        pl.when(receives)(item.wait_recv)
    rim_turn = lax.rem(row, 3)
    for x in range(ex):
        field_ref[here + x, 3] = jnp.where(
            rim_turn == 2,
            near_rim[0, x].astype(jnp.float32),
            near_rim[1, x].astype(jnp.float32),
        ).astype(jnp.bfloat16)

    def start_edge(d, carry):
        edge_copy(f, d, lax.rem(f + d, slabs)).start()
        return carry

    lax.fori_loop(1, slabs, start_edge, 0)

    def forward(d, carry):
        slab = lax.rem(f + slabs - d, slabs)
        field_copy(slab, d, f).wait_recv()
        edge_copy(slab, d, f).wait_recv()
        forward_copy(slab, d, t).start()
        return carry

    lax.fori_loop(1, slabs, forward, 0)

    def finish(d, carry):
        slab = lax.rem(f + slabs - d, slabs)
        forward_copy(slab, d, 1 - t).wait_recv()
        forward_copy(slab, d, t).wait_send()
        field_copy(f, d, lax.rem(f + d, slabs)).wait_send()
        edge_copy(f, d, lax.rem(f + d, slabs)).wait_send()
        slab_copy(d).wait_send()
        return carry

    lax.fori_loop(1, slabs, finish, 0)

    def sent_pair(d, carry):
        pair_copy(d).wait_send()
        return carry

    lax.fori_loop(0, slabs, sent_pair, 0)
    total_copy.wait_send()
    for copies in (x_copies, y_copies, near_copies):
        for sends, _, item, _ in copies:
            pl.when(sends)(item.wait_send)
    for sends, slot in ((has_high, 0), (has_low, 1)):

        @pl.when(sends)
        def _(slot=slot):
            for core in range(2):
                pltpu.make_async_remote_copy(
                    src_ref=total.at[t, :, 3],
                    dst_ref=rims.at[slot, t],
                    send_sem=sem_rim.at[0, slot, core],
                    recv_sem=sem_rim.at[1, slot, t],
                    device_id=other,
                    device_id_type=MESH,
                ).wait_send()


def body(slabs, subs, velocity, pressure, viscosity, marker_force, marker_offset, cell_base,
         block_slab):
    ex, ey, _, depth = velocity.shape
    hx = ex // 2
    blocks, _, markers = marker_force.shape
    width = slabs * ex + REACH
    bf16, f32 = jnp.bfloat16, jnp.float32
    vmem = pl.BlockSpec(memory_space=pltpu.VMEM)
    smem = pl.BlockSpec(memory_space=pltpu.SMEM)
    tile = ey * depth
    field_bytes = width * 4 * tile * 2
    target = block_slab[:, 0]

    parts = pl.pallas_call(
        functools.partial(spread_kernel, ex, ey),
        out_shape=jax.ShapeDtypeStruct((slabs * ex, 4, ey, depth), bf16),
        in_specs=[smem, vmem, vmem, vmem],
        out_specs=vmem,
        scratch_shapes=[pltpu.VMEM((width, 3, ey + RIM, depth), f32)],
        compiler_params=pltpu.CompilerParams(
            vmem_limit_bytes=width * 3 * (ey + RIM) * depth * 4 + field_bytes + 12 * MIB
        ),
        name="spread",
    )(target, marker_force, marker_offset, cell_base)

    old = jnp.concatenate(
        [jnp.transpose(velocity, (0, 2, 1, 3)), pressure[:, None], viscosity[:, None]], axis=1
    )
    dma = pltpu.SemaphoreType.DMA
    half = (hx, 4, ey, depth)
    fresh, field = pl.pallas_call(
        functools.partial(grid_kernel, slabs, subs),
        out_shape=(
            jax.ShapeDtypeStruct((ex, 3, ey, depth), f32),
            jax.ShapeDtypeStruct((width, 4, ey, depth), bf16),
        ),
        in_specs=[vmem, vmem],
        out_specs=(vmem, vmem),
        scratch_shapes=[
            pltpu.VMEM((slabs,) + half, bf16),
            pltpu.VMEM((slabs,) + half, bf16),
            pltpu.VMEM((slabs,) + half, bf16),
            pltpu.VMEM((2,) + half, f32),
            pltpu.VMEM((2, 2, hx, ey, depth), f32),
            pltpu.VMEM((2, 5, ey, depth), f32),
            pltpu.VMEM((2, ex, 5, 8, depth), f32),
            pltpu.VMEM((ex, ey, depth), bf16),
            pltpu.VMEM((2, ex, ey, depth), bf16),
            dma((2, slabs)),
            dma((2, slabs)),
            dma((2, 2)),
            dma((2, 2, 2)),
            dma((2, 2)),
            dma((2, 2)),
            dma((2, 2)),
            dma((2, slabs)),
            dma((2, slabs)),
            dma((2, slabs)),
        ],
        compiler_params=pltpu.CompilerParams(
            collective_id=0,
            has_side_effects=True,
            vmem_limit_bytes=4 * field_bytes + 12 * MIB,
        ),
        name="grid",
    )(old, parts.reshape((slabs, 2) + half))

    marker_velocity = pl.pallas_call(
        functools.partial(sample_kernel, ex, ey),
        out_shape=jax.ShapeDtypeStruct((blocks, 3, markers), f32),
        in_specs=[smem, vmem, vmem, vmem],
        out_specs=vmem,
        compiler_params=pltpu.CompilerParams(vmem_limit_bytes=field_bytes + 12 * MIB),
        name="sample",
    )(target, marker_offset, cell_base, field)
    return (jnp.transpose(fresh, (0, 2, 1, 3)), marker_velocity)


def solution(mesh):
    marker = P(("fluid", "sub", "struct"), None, None)
    return jax.shard_map(
        functools.partial(body, mesh.shape["fluid"], mesh.shape["sub"]),
        mesh=mesh,
        in_specs=(
            P("fluid", "sub", None, None),
            P("fluid", "sub", None),
            P("fluid", "sub", None),
            marker,
            marker,
            marker,
            P(("fluid", "sub", "struct"), None),
        ),
        out_specs=(P("fluid", "sub", None, None), marker),
        check_vma=False,
    )
```

```python
import functools

import jax
import jax.numpy as jnp
from jax import lax
from jax.experimental import pallas as pl
from jax.experimental.pallas import tpu as pltpu
from jax.sharding import PartitionSpec as P

MESH = pl.DeviceIdType.MESH
RIM = 8
REACH = 3
MIB = 1 << 20
UNROLL = 8


def stencil(offsets):
    root = jnp.sqrt(1.0 + 4.0 * offsets - 4.0 * offsets * offsets)
    low = 3.0 - 2.0 * offsets
    high = 1.0 + 2.0 * offsets
    return (
        (low - root) * 0.125,
        (low + root) * 0.125,
        (high + root) * 0.125,
        (high - root) * 0.125,
    )


def place(weights, shift):
    result = jnp.zeros(shift.shape, jnp.float32)
    for n in range(4):
        result = jnp.where(shift == n - 1, weights[n], result)
    return result


def at_cells(base, depth, markers):
    cells = lax.broadcasted_iota(jnp.int32, (depth, markers), 0).astype(jnp.int16)
    shift = cells - jnp.broadcast_to(base, (16, markers)).astype(jnp.int16)[0:1]
    return [shift == jnp.int16(n - 1) for n in range(4)]


def choose(where, values):
    result = jnp.zeros(where[0].shape, jnp.bfloat16)
    for mask, value in zip(where, values):
        value = jnp.broadcast_to(value, (16, value.shape[1])).astype(jnp.bfloat16)[0:1]
        result = jnp.where(mask, value, result)
    return result


def spread_kernel(ex, ey, slab_ref, force_ref, offset_ref, base_ref, out_ref, acc, held, loads):
    _, blocks, markers = force_ref.shape
    depth = acc.shape[3]
    rows = ey + RIM
    span = ex + REACH
    acc[...] = jnp.zeros_like(acc)
    for axis in range(3):
        for n, weight in enumerate(stencil(offset_ref[axis])):
            if axis < 2:
                held[axis, n] = weight
            else:
                for c in range(3):
                    loads[c, n] = force_ref[c] * weight
    xs = lax.broadcasted_iota(jnp.int32, (span, markers), 0) - 1
    ys = lax.broadcasted_iota(jnp.int32, (rows, markers), 0)
    ys = jnp.where(ys == ey + 2, -1, jnp.where(ys > ey + 2, -100, ys))

    def step(b, carry):
        start = slab_ref[b] * ex
        one = pl.ds(b, 1)
        wx = place([held[0, n, one] for n in range(4)], xs - base_ref[0, one])
        wy = place([held[1, n, one] for n in range(4)], ys - base_ref[1, one])
        where = at_cells(base_ref[2, one], depth, markers)
        plane = jnp.concatenate([wx[i : i + 1] * wy for i in range(span)], axis=0)
        plane = plane.astype(jnp.bfloat16)
        for c in range(3):
            loaded = choose(where, [loads[c, n, one] for n in range(4)])
            term = lax.dot_general(
                plane, loaded, (((1,), (1,)), ((), ())), preferred_element_type=jnp.float32
            )
            acc[pl.ds(start, span), c] += term.reshape(span, rows, depth)
        return carry

    lax.fori_loop(0, blocks, step, 0, unroll=UNROLL)

    def pack(x, carry):
        for c in range(3):
            out_ref[x, c] = acc[x + 1, c, 0:ey, :].astype(jnp.bfloat16)
        parts = [acc[x + 1, c, ey : ey + 3, :] for c in range(3)]
        parts.append(jnp.zeros((ey - 9, depth), jnp.float32))
        out_ref[x, 3] = jnp.concatenate(parts, axis=0).astype(jnp.bfloat16)
        return carry

    lax.fori_loop(0, out_ref.shape[0], pack, 0)


def sample_kernel(
    ex, ey, slab_ref, offset_ref, base_ref, field_ref, new_ref, out_ref, fresh_ref, held
):
    _, blocks, markers = offset_ref.shape
    depth = field_ref.shape[3]
    span = ex + REACH
    fresh_ref[...] = new_ref[...]
    for axis in range(3):
        for n, weight in enumerate(stencil(offset_ref[axis])):
            held[axis, n] = weight
    xs = lax.broadcasted_iota(jnp.int32, (span, markers), 0) - 1
    ys = lax.broadcasted_iota(jnp.int32, (ey, markers), 0)
    turn = ys % 3
    rim = jnp.where(ys >= 9, -100, jnp.where(turn == 2, -1, ey + turn))

    def step(b, carry):
        start = slab_ref[b] * ex
        one = pl.ds(b, 1)
        weights = [[held[axis, n, one] for n in range(4)] for axis in range(3)]
        wx = place(weights[0], xs - base_ref[0, one])
        wy = place(weights[1], ys - base_ref[1, one])
        wr = place(weights[1], rim - base_ref[1, one])
        where = at_cells(base_ref[2, one], depth, markers)
        wz = choose(where, weights[2])
        cells = field_ref[pl.ds(start, span)].reshape(span * 4 * ey, depth)
        sums = jnp.dot(cells, wz, preferred_element_type=jnp.float32)
        sums = sums.reshape(span, 4 * ey, markers)
        across = sums[0] * wx[0:1]
        for i in range(1, span):
            across = across + sums[i] * wx[i : i + 1]
        edge = across[3 * ey : 4 * ey] * wr
        for c in range(3):
            own = jnp.sum(across[c * ey : (c + 1) * ey] * wy, axis=0, keepdims=True)
            beside = jnp.sum(edge[3 * c : 3 * c + 3], axis=0, keepdims=True)
            out_ref[c, one] = own + beside
        return carry

    lax.fori_loop(0, blocks, step, 0, unroll=UNROLL)


def grid_kernel(
    slabs, subs,
    old_ref, part_ref, fresh_ref, field_ref,
    pair, outgoing, incoming, total, rims, xhalo, yhalo, my_rim, near_rim,
    sem_pair, sem_slab, sem_total, sem_rim, sem_x, sem_y, sem_near,
    sem_field, sem_edge, sem_forward,
):
    f, s, t = lax.axis_index("fluid"), lax.axis_index("sub"), lax.axis_index("struct")
    ex, _, ey, depth = old_ref.shape
    hx = ex // 2
    other = (f, s, 1 - t)
    has_low, has_high = s > 0, s < subs - 1
    has_left, has_right = f > 0, f < slabs - 1

    def copy(src, dst, sems, index, device):
        return pltpu.make_async_remote_copy(
            src_ref=src,
            dst_ref=dst,
            send_sem=sems.at[(0,) + index],
            recv_sem=sems.at[(1,) + index],
            device_id=device,
            device_id_type=MESH,
        )

    barrier = pltpu.get_barrier_semaphore()

    def greet(device):
        pl.semaphore_signal(barrier, inc=1, device_id=device, device_id_type=MESH)

    greet(other)

    def greet_slab(d, carry):
        greet((lax.rem(f + d, slabs), s, t))
        return carry

    lax.fori_loop(1, slabs, greet_slab, 0)
    for present, step in ((has_low, -1), (has_high, 1)):

        @pl.when(present)
        def _(step=step):
            greet((f, s + step, t))
            greet((f, s + step, 1 - t))

    beside = has_low.astype(jnp.int32) + has_high.astype(jnp.int32)
    pl.semaphore_wait(barrier, slabs + 2 * beside)

    def pair_copy(slab):
        return copy(part_ref.at[slab, 1 - t], pair.at[slab], sem_pair, (slab,), other)

    def start_pair(d, carry):
        pair_copy(lax.rem(f + d, slabs)).start()
        return carry

    lax.fori_loop(1, slabs + 1, start_pair, 0)

    x_copies = (
        (has_left, has_right, copy(old_ref.at[0], xhalo.at[1], sem_x, (1,), (f - 1, s, t)), 1),
        (has_right, has_left, copy(old_ref.at[ex - 1], xhalo.at[0], sem_x, (0,), (f + 1, s, t)), 0),
    )
    y_copies = (
        (has_low, has_high,
         copy(old_ref.at[:, :, 0:8], yhalo.at[1], sem_y, (1,), (f, s - 1, t)), 1),
        (has_high, has_low,
         copy(old_ref.at[:, :, ey - 8 : ey], yhalo.at[0], sem_y, (0,), (f, s + 1, t)), 0),
    )
    for copies, halo in ((x_copies, xhalo), (y_copies, yhalo)):
        for sends, receives, item, slot in copies:
            pl.when(sends)(item.start)

            @pl.when(jnp.logical_not(receives))
            def _(halo=halo, slot=slot):
                halo[slot] = jnp.zeros(halo.shape[1:], halo.dtype)

    def slab_copy(d):
        return copy(
            outgoing.at[d], incoming.at[d], sem_slab, (d,), (lax.rem(f + d, slabs), s, t)
        )

    def send_slab(d, carry):
        slab = lax.rem(f + d, slabs)
        pair_copy(slab).wait_recv()
        both = part_ref[slab, t].astype(jnp.float32) + pair[slab].astype(jnp.float32)
        outgoing[d] = both.astype(jnp.bfloat16)
        slab_copy(d).start()
        return carry

    lax.fori_loop(1, slabs, send_slab, 0)
    pair_copy(f).wait_recv()
    total[t] = part_ref[f, t].astype(jnp.float32) + pair[f].astype(jnp.float32)

    def add_slab(d, carry):
        slab_copy(d).wait_recv()
        total[t] += incoming[d].astype(jnp.float32)
        return carry

    lax.fori_loop(1, slabs, add_slab, 0)

    total_copy = copy(total.at[t], total.at[t], sem_total, (t,), other)
    total_back = copy(total.at[1 - t], total.at[1 - t], sem_total, (1 - t,), other)
    total_copy.start()
    for sends, receives, step, slot in ((has_high, has_low, 1, 0), (has_low, has_high, -1, 1)):

        @pl.when(sends)
        def _(step=step, slot=slot):
            for core in range(2):
                to = lax.rem(t + core, 2)
                pltpu.make_async_remote_copy(
                    src_ref=total.at[t, :, 3],
                    dst_ref=rims.at[slot, t],
                    send_sem=sem_rim.at[0, slot, core],
                    recv_sem=sem_rim.at[1, slot, t],
                    device_id=(f, s + step, to),
                    device_id_type=MESH,
                ).start()

        @pl.when(jnp.logical_not(receives))
        def _(slot=slot):
            rims[slot] = jnp.zeros(rims.shape[1:], rims.dtype)

    for copies in (x_copies, y_copies):
        for _, receives, item, _ in copies:
            pl.when(receives)(item.wait_recv)
    total_back.wait_recv()
    for receives, slot in ((has_low, 0), (has_high, 1)):

        @pl.when(receives)
        def _(slot=slot):
            for core in range(2):
                pltpu.make_async_remote_copy(
                    src_ref=total.at[t, :, 3],
                    dst_ref=rims.at[slot, core],
                    send_sem=sem_rim.at[0, slot, core],
                    recv_sem=sem_rim.at[1, slot, core],
                    device_id=other,
                    device_id_type=MESH,
                ).wait_recv()

    row = lax.broadcasted_iota(jnp.int32, (ey, depth), 0)
    lane = lax.broadcasted_iota(jnp.int32, (ey, depth), 1)
    here = 1 + ex * f

    def around(x, i):
        mid = old_ref[x, i]
        return (
            mid,
            old_ref[x + 1, i] if x < ex - 1 else xhalo[1, i],
            old_ref[x - 1, i] if x > 0 else xhalo[0, i],
            jnp.where(row == ey - 1, yhalo[1, x, i, 0:1, :], pltpu.roll(mid, ey - 1, 0)),
            jnp.where(row == 0, yhalo[0, x, i, 7:8, :], pltpu.roll(mid, 1, 0)),
            jnp.where(lane == depth - 1, 0.0, pltpu.roll(mid, depth - 1, 1)),
            jnp.where(lane == 0, 0.0, pltpu.roll(mid, 1, 1)),
        )

    for x in range(ex):
        pressure = around(x, 3)
        viscosity = around(x, 4)
        faces = [0.5 * (viscosity[0] + beside) for beside in viscosity[1:]]
        half, xi = x // hx, x % hx
        edge_rows = []
        for c in range(3):
            old = around(x, c)
            viscous = jnp.zeros((ey, depth), jnp.float32)
            for n in range(6):
                viscous = viscous + faces[n] * (old[n + 1] - old[0])
            slope = pressure[1 + 2 * c] - pressure[0]
            force = total[half, xi, c]
            low0 = rims[0, half, xi, 3 * c : 3 * c + 1, :]
            low1 = rims[0, half, xi, 3 * c + 1 : 3 * c + 2, :]
            top = rims[1, half, xi, 3 * c + 2 : 3 * c + 3, :]
            force = force + jnp.where(
                row == 0, low0, jnp.where(row == 1, low1, jnp.where(row == ey - 1, top, 0.0))
            )
            new = old[0] + 0.5 * (viscous - slope + force)
            fresh_ref[x, c] = new
            field_ref[here + x, c] = new.astype(jnp.bfloat16)
            edge_rows += [new[0:2], new[ey - 1 : ey]]
        edge_rows.append(jnp.zeros((ey - 9, depth), jnp.float32))
        my_rim[x] = jnp.concatenate(edge_rows, axis=0).astype(jnp.bfloat16)

    near_copies = (
        (has_high, has_low, copy(my_rim, near_rim.at[0], sem_near, (0,), (f, s + 1, t)), 0),
        (has_low, has_high, copy(my_rim, near_rim.at[1], sem_near, (1,), (f, s - 1, t)), 1),
    )
    for sends, receives, item, slot in near_copies:
        pl.when(sends)(item.start)

        @pl.when(jnp.logical_not(receives))
        def _(slot=slot):
            near_rim[slot] = jnp.zeros(near_rim.shape[1:], near_rim.dtype)

    def field_copy(slab, d, to):
        part = field_ref.at[pl.ds(1 + ex * slab + hx * t, hx), 0:3]
        return copy(part, part, sem_field, (d,), (to, s, t))

    def edge_copy(slab, d, to):
        part = field_ref.at[pl.ds(1 + ex * slab + hx * t, hx), 3]
        return copy(part, part, sem_edge, (d,), (to, s, t))

    def forward_copy(slab, d, core):
        part = field_ref.at[pl.ds(1 + ex * slab + hx * core, hx)]
        return copy(part, part, sem_forward, (d,), other)

    def start_field(d, carry):
        field_copy(f, d, lax.rem(f + d, slabs)).start()
        return carry

    lax.fori_loop(1, slabs, start_field, 0)
    for outside in (0, slabs * ex + 1, slabs * ex + 2):
        field_ref[outside] = jnp.zeros(field_ref.shape[1:], field_ref.dtype)
    for sends, receives, item, slot in near_copies:
        pl.when(receives)(item.wait_recv)
    rim_turn = lax.rem(row, 3)
    for x in range(ex):
        field_ref[here + x, 3] = jnp.where(
            rim_turn == 2,
            near_rim[0, x].astype(jnp.float32),
            near_rim[1, x].astype(jnp.float32),
        ).astype(jnp.bfloat16)

    def start_edge(d, carry):
        edge_copy(f, d, lax.rem(f + d, slabs)).start()
        return carry

    lax.fori_loop(1, slabs, start_edge, 0)

    def forward(d, carry):
        slab = lax.rem(f + slabs - d, slabs)
        field_copy(slab, d, f).wait_recv()
        edge_copy(slab, d, f).wait_recv()
        forward_copy(slab, d, t).start()
        return carry

    lax.fori_loop(1, slabs, forward, 0)

    def finish(d, carry):
        slab = lax.rem(f + slabs - d, slabs)
        forward_copy(slab, d, 1 - t).wait_recv()
        forward_copy(slab, d, t).wait_send()
        field_copy(f, d, lax.rem(f + d, slabs)).wait_send()
        edge_copy(f, d, lax.rem(f + d, slabs)).wait_send()
        slab_copy(d).wait_send()
        return carry

    lax.fori_loop(1, slabs, finish, 0)

    def sent_pair(d, carry):
        pair_copy(d).wait_send()
        return carry

    lax.fori_loop(0, slabs, sent_pair, 0)
    total_copy.wait_send()
    for copies in (x_copies, y_copies, near_copies):
        for sends, _, item, _ in copies:
            pl.when(sends)(item.wait_send)
    for sends, slot in ((has_high, 0), (has_low, 1)):

        @pl.when(sends)
        def _(slot=slot):
            for core in range(2):
                pltpu.make_async_remote_copy(
                    src_ref=total.at[t, :, 3],
                    dst_ref=rims.at[slot, t],
                    send_sem=sem_rim.at[0, slot, core],
                    recv_sem=sem_rim.at[1, slot, t],
                    device_id=other,
                    device_id_type=MESH,
                ).wait_send()


def body(slabs, subs, velocity, pressure, viscosity, marker_force, marker_offset, cell_base,
         block_slab):
    ex, ey, _, depth = velocity.shape
    hx = ex // 2
    blocks, _, markers = marker_force.shape
    width = slabs * ex + REACH
    bf16, f32 = jnp.bfloat16, jnp.float32
    vmem = pl.BlockSpec(memory_space=pltpu.VMEM)
    smem = pl.BlockSpec(memory_space=pltpu.SMEM)
    tile = ey * depth
    field_bytes = width * 4 * tile * 2
    target = block_slab[:, 0]
    forces, offsets, bases = (
        jnp.transpose(a, (1, 0, 2)) for a in (marker_force, marker_offset, cell_base)
    )

    parts = pl.pallas_call(
        functools.partial(spread_kernel, ex, ey),
        out_shape=jax.ShapeDtypeStruct((slabs * ex, 4, ey, depth), bf16),
        in_specs=[smem, vmem, vmem, vmem],
        out_specs=vmem,
        scratch_shapes=[
            pltpu.VMEM((width, 3, ey + RIM, depth), f32),
            pltpu.VMEM((2, 4, blocks, markers), f32),
            pltpu.VMEM((3, 4, blocks, markers), f32),
        ],
        compiler_params=pltpu.CompilerParams(
            vmem_limit_bytes=width * 3 * (ey + RIM) * depth * 4 + field_bytes + 12 * MIB
        ),
        name="spread",
    )(target, forces, offsets, bases)

    old = jnp.concatenate(
        [jnp.transpose(velocity, (0, 2, 1, 3)), pressure[:, None], viscosity[:, None]], axis=1
    )
    dma = pltpu.SemaphoreType.DMA
    half = (hx, 4, ey, depth)
    fresh, field = pl.pallas_call(
        functools.partial(grid_kernel, slabs, subs),
        out_shape=(
            jax.ShapeDtypeStruct((ex, 3, ey, depth), f32),
            jax.ShapeDtypeStruct((width, 4, ey, depth), bf16),
        ),
        in_specs=[vmem, vmem],
        out_specs=(vmem, vmem),
        scratch_shapes=[
            pltpu.VMEM((slabs,) + half, bf16),
            pltpu.VMEM((slabs,) + half, bf16),
            pltpu.VMEM((slabs,) + half, bf16),
            pltpu.VMEM((2,) + half, f32),
            pltpu.VMEM((2, 2, hx, ey, depth), f32),
            pltpu.VMEM((2, 5, ey, depth), f32),
            pltpu.VMEM((2, ex, 5, 8, depth), f32),
            pltpu.VMEM((ex, ey, depth), bf16),
            pltpu.VMEM((2, ex, ey, depth), bf16),
            dma((2, slabs)),
            dma((2, slabs)),
            dma((2, 2)),
            dma((2, 2, 2)),
            dma((2, 2)),
            dma((2, 2)),
            dma((2, 2)),
            dma((2, slabs)),
            dma((2, slabs)),
            dma((2, slabs)),
        ],
        compiler_params=pltpu.CompilerParams(
            collective_id=0,
            has_side_effects=True,
            vmem_limit_bytes=4 * field_bytes + 12 * MIB,
        ),
        name="grid",
    )(old, parts.reshape((slabs, 2) + half))

    marker_velocity, fresh = pl.pallas_call(
        functools.partial(sample_kernel, ex, ey),
        out_shape=(
            jax.ShapeDtypeStruct((3, blocks, markers), f32),
            jax.ShapeDtypeStruct(fresh.shape, f32),
        ),
        in_specs=[smem, vmem, vmem, vmem, vmem],
        out_specs=(vmem, vmem),
        scratch_shapes=[pltpu.VMEM((3, 4, blocks, markers), f32)],
        compiler_params=pltpu.CompilerParams(vmem_limit_bytes=field_bytes + 12 * MIB),
        name="sample",
    )(target, offsets, bases, field, fresh)
    return (jnp.transpose(fresh, (0, 2, 1, 3)), jnp.transpose(marker_velocity, (1, 0, 2)))


def solution(mesh):
    marker = P(("fluid", "sub", "struct"), None, None)
    return jax.shard_map(
        functools.partial(body, mesh.shape["fluid"], mesh.shape["sub"]),
        mesh=mesh,
        in_specs=(
            P("fluid", "sub", None, None),
            P("fluid", "sub", None),
            P("fluid", "sub", None),
            marker,
            marker,
            marker,
            P(("fluid", "sub", "struct"), None),
        ),
        out_specs=(P("fluid", "sub", None, None), marker),
        check_vma=False,
    )
```

```python
import functools

import jax
import jax.numpy as jnp
from jax import lax
from jax.experimental import pallas as pl
from jax.experimental.pallas import tpu as pltpu
from jax.sharding import PartitionSpec as P

MESH = pl.DeviceIdType.MESH
RIM = 8
REACH = 3
MIB = 1 << 20
UNROLL = 8


def stencil(offsets):
    root = jnp.sqrt(1.0 + 4.0 * offsets - 4.0 * offsets * offsets)
    low = 3.0 - 2.0 * offsets
    high = 1.0 + 2.0 * offsets
    return (
        (low - root) * 0.125,
        (low + root) * 0.125,
        (high + root) * 0.125,
        (high - root) * 0.125,
    )


def place(weights, shift):
    result = jnp.zeros(shift.shape, jnp.float32)
    for n in range(4):
        result = jnp.where(shift == n - 1, weights[n], result)
    return result


def at_cells(base, depth, markers):
    cells = lax.broadcasted_iota(jnp.int32, (depth, markers), 0).astype(jnp.int16)
    shift = cells - jnp.broadcast_to(base, (16, markers)).astype(jnp.int16)[0:1]
    return [shift == jnp.int16(n - 1) for n in range(4)]


def choose(where, values):
    result = jnp.zeros(where[0].shape, jnp.bfloat16)
    for mask, value in zip(where, values):
        value = jnp.broadcast_to(value, (16, value.shape[1])).astype(jnp.bfloat16)[0:1]
        result = jnp.where(mask, value, result)
    return result


def spread_kernel(ex, ey, slab_ref, force_ref, offset_ref, base_ref, out_ref, acc, held, loads):
    _, blocks, markers = force_ref.shape
    depth = acc.shape[3]
    rows = ey + RIM
    span = ex + REACH
    acc[...] = jnp.zeros_like(acc)
    for axis in range(3):
        for n, weight in enumerate(stencil(offset_ref[axis])):
            if axis < 2:
                held[axis, n] = weight
            else:
                for c in range(3):
                    loads[c, n] = force_ref[c] * weight
    xs = lax.broadcasted_iota(jnp.int32, (span, markers), 0) - 1
    ys = lax.broadcasted_iota(jnp.int32, (rows, markers), 0)
    ys = jnp.where(ys == ey + 2, -1, jnp.where(ys > ey + 2, -100, ys))

    def step(b, carry):
        start = slab_ref[b] * ex
        one = pl.ds(b, 1)
        wx = place([held[0, n, one] for n in range(4)], xs - base_ref[0, one])
        wy = place([held[1, n, one] for n in range(4)], ys - base_ref[1, one])
        where = at_cells(base_ref[2, one], depth, markers)
        plane = jnp.concatenate([wx[i : i + 1] * wy for i in range(span)], axis=0)
        plane = plane.astype(jnp.bfloat16)
        for c in range(3):
            loaded = choose(where, [loads[c, n, one] for n in range(4)])
            term = lax.dot_general(
                plane, loaded, (((1,), (1,)), ((), ())), preferred_element_type=jnp.float32
            )
            acc[pl.ds(start, span), c] += term.reshape(span, rows, depth)
        return carry

    lax.fori_loop(0, blocks, step, 0, unroll=UNROLL)

    def pack(x, carry):
        for c in range(3):
            out_ref[x, c] = acc[x + 1, c, 0:ey, :].astype(jnp.bfloat16)
        parts = [acc[x + 1, c, ey : ey + 3, :] for c in range(3)]
        parts.append(jnp.zeros((ey - 9, depth), jnp.float32))
        out_ref[x, 3] = jnp.concatenate(parts, axis=0).astype(jnp.bfloat16)
        return carry

    lax.fori_loop(0, out_ref.shape[0], pack, 0)


def sample_kernel(
    ex, ey, slab_ref, offset_ref, base_ref, field_ref, new_ref, out_ref, fresh_ref, held
):
    _, blocks, markers = offset_ref.shape
    depth = field_ref.shape[3]
    span = ex + REACH
    fresh_ref[...] = new_ref[...]
    for axis in range(3):
        for n, weight in enumerate(stencil(offset_ref[axis])):
            held[axis, n] = weight
    xs = lax.broadcasted_iota(jnp.int32, (span, markers), 0) - 1
    ys = lax.broadcasted_iota(jnp.int32, (ey, markers), 0)
    turn = ys % 3
    rim = jnp.where(ys >= 9, -100, jnp.where(turn == 2, -1, ey + turn))

    def step(b, carry):
        start = slab_ref[b] * ex
        one = pl.ds(b, 1)
        weights = [[held[axis, n, one] for n in range(4)] for axis in range(3)]
        wx = place(weights[0], xs - base_ref[0, one])
        wy = place(weights[1], ys - base_ref[1, one])
        wr = place(weights[1], rim - base_ref[1, one])
        where = at_cells(base_ref[2, one], depth, markers)
        wz = choose(where, weights[2])
        cells = field_ref[pl.ds(start, span)].reshape(span * 4 * ey, depth)
        sums = jnp.dot(cells, wz, preferred_element_type=jnp.float32)
        sums = sums.reshape(span, 4 * ey, markers)
        across = sums[0] * wx[0:1]
        for i in range(1, span):
            across = across + sums[i] * wx[i : i + 1]
        edge = across[3 * ey : 4 * ey] * wr
        for c in range(3):
            own = jnp.sum(across[c * ey : (c + 1) * ey] * wy, axis=0, keepdims=True)
            beside = jnp.sum(edge[3 * c : 3 * c + 3], axis=0, keepdims=True)
            out_ref[c, one] = own + beside
        return carry

    lax.fori_loop(0, blocks, step, 0, unroll=UNROLL)


def grid_kernel(
    slabs, subs,
    velocity_ref, pressure_ref, viscosity_ref, part_ref, fresh_ref, field_ref,
    old_ref, pair, outgoing, incoming, total, rims, yhalo, my_rim, near_rim,
    sem_pair, sem_slab, sem_total, sem_rim, sem_x, sem_y, sem_near,
    sem_field, sem_edge, sem_forward,
):
    f, s, t = lax.axis_index("fluid"), lax.axis_index("sub"), lax.axis_index("struct")
    ex, _, ey, depth = velocity_ref.shape
    hx = ex // 2
    other = (f, s, 1 - t)
    has_low, has_high = s > 0, s < subs - 1
    has_left, has_right = f > 0, f < slabs - 1

    def copy(src, dst, sems, index, device):
        return pltpu.make_async_remote_copy(
            src_ref=src,
            dst_ref=dst,
            send_sem=sems.at[(0,) + index],
            recv_sem=sems.at[(1,) + index],
            device_id=device,
            device_id_type=MESH,
        )

    barrier = pltpu.get_barrier_semaphore()

    def greet(device):
        pl.semaphore_signal(barrier, inc=1, device_id=device, device_id_type=MESH)

    greet(other)

    def greet_slab(d, carry):
        greet((lax.rem(f + d, slabs), s, t))
        return carry

    lax.fori_loop(1, slabs, greet_slab, 0)
    for present, step in ((has_low, -1), (has_high, 1)):

        @pl.when(present)
        def _(step=step):
            greet((f, s + step, t))
            greet((f, s + step, 1 - t))

    old_ref[1 : ex + 1, 0:3] = velocity_ref[...]
    old_ref[1 : ex + 1, 3] = pressure_ref[...]
    old_ref[1 : ex + 1, 4] = viscosity_ref[...]
    beside = has_low.astype(jnp.int32) + has_high.astype(jnp.int32)
    pl.semaphore_wait(barrier, slabs + 2 * beside)

    def pair_copy(slab):
        return copy(part_ref.at[slab, 1 - t], pair.at[slab], sem_pair, (slab,), other)

    def start_pair(d, carry):
        pair_copy(lax.rem(f + d, slabs)).start()
        return carry

    lax.fori_loop(1, slabs + 1, start_pair, 0)

    x_copies = (
        (has_left, has_right,
         copy(old_ref.at[1], old_ref.at[ex + 1], sem_x, (1,), (f - 1, s, t)), old_ref, ex + 1),
        (has_right, has_left,
         copy(old_ref.at[ex], old_ref.at[0], sem_x, (0,), (f + 1, s, t)), old_ref, 0),
    )
    y_copies = (
        (has_low, has_high,
         copy(old_ref.at[1 : ex + 1, :, 0:8], yhalo.at[1], sem_y, (1,), (f, s - 1, t)), yhalo, 1),
        (has_high, has_low,
         copy(old_ref.at[1 : ex + 1, :, ey - 8 : ey], yhalo.at[0], sem_y, (0,), (f, s + 1, t)),
         yhalo, 0),
    )
    for sends, receives, item, halo, slot in x_copies + y_copies:
        pl.when(sends)(item.start)

        @pl.when(jnp.logical_not(receives))
        def _(halo=halo, slot=slot):
            halo[slot] = jnp.zeros(halo.shape[1:], halo.dtype)

    def slab_copy(d):
        return copy(
            outgoing.at[d], incoming.at[d], sem_slab, (d,), (lax.rem(f + d, slabs), s, t)
        )

    def send_slab(d, carry):
        slab = lax.rem(f + d, slabs)
        pair_copy(slab).wait_recv()
        both = part_ref[slab, t].astype(jnp.float32) + pair[slab].astype(jnp.float32)
        outgoing[d] = both.astype(jnp.bfloat16)
        slab_copy(d).start()
        return carry

    lax.fori_loop(1, slabs, send_slab, 0)
    pair_copy(f).wait_recv()
    total[t] = part_ref[f, t].astype(jnp.float32) + pair[f].astype(jnp.float32)

    def add_slab(d, carry):
        slab_copy(d).wait_recv()
        total[t] += incoming[d].astype(jnp.float32)
        return carry

    lax.fori_loop(1, slabs, add_slab, 0)

    total_copy = copy(total.at[t], total.at[t], sem_total, (t,), other)
    total_back = copy(total.at[1 - t], total.at[1 - t], sem_total, (1 - t,), other)
    total_copy.start()
    for sends, receives, step, slot in ((has_high, has_low, 1, 0), (has_low, has_high, -1, 1)):

        @pl.when(sends)
        def _(step=step, slot=slot):
            for core in range(2):
                to = lax.rem(t + core, 2)
                pltpu.make_async_remote_copy(
                    src_ref=total.at[t, :, 3],
                    dst_ref=rims.at[slot, t],
                    send_sem=sem_rim.at[0, slot, core],
                    recv_sem=sem_rim.at[1, slot, t],
                    device_id=(f, s + step, to),
                    device_id_type=MESH,
                ).start()

        @pl.when(jnp.logical_not(receives))
        def _(slot=slot):
            rims[slot] = jnp.zeros(rims.shape[1:], rims.dtype)

    for _, receives, item, _, _ in x_copies + y_copies:
        pl.when(receives)(item.wait_recv)
    total_back.wait_recv()
    for receives, slot in ((has_low, 0), (has_high, 1)):

        @pl.when(receives)
        def _(slot=slot):
            for core in range(2):
                pltpu.make_async_remote_copy(
                    src_ref=total.at[t, :, 3],
                    dst_ref=rims.at[slot, core],
                    send_sem=sem_rim.at[0, slot, core],
                    recv_sem=sem_rim.at[1, slot, core],
                    device_id=other,
                    device_id_type=MESH,
                ).wait_recv()

    row = lax.broadcasted_iota(jnp.int32, (ey, depth), 0)
    lane = lax.broadcasted_iota(jnp.int32, (ey, depth), 1)
    here = 1 + ex * f

    def around(x, i):
        mid = old_ref[x + 1, i]
        return (
            mid,
            old_ref[x + 2, i],
            old_ref[x, i],
            jnp.where(row == ey - 1, yhalo[1, x, i, 0:1, :], pltpu.roll(mid, ey - 1, 0)),
            jnp.where(row == 0, yhalo[0, x, i, 7:8, :], pltpu.roll(mid, 1, 0)),
            jnp.where(lane == depth - 1, 0.0, pltpu.roll(mid, depth - 1, 1)),
            jnp.where(lane == 0, 0.0, pltpu.roll(mid, 1, 1)),
        )

    def field_copy(slab, d, to):
        part = field_ref.at[pl.ds(1 + ex * slab + hx * t, hx), 0:3]
        return copy(part, part, sem_field, (d,), (to, s, t))

    def start_field(d, carry):
        field_copy(f, d, lax.rem(f + d, slabs)).start()
        return carry

    for i in range(ex):
        x = lax.rem(hx * t + i, ex)
        pressure = around(x, 3)
        viscosity = around(x, 4)
        faces = [0.5 * (viscosity[0] + beside) for beside in viscosity[1:]]
        half, xi = (t, i) if i < hx else (1 - t, i - hx)
        edge_rows = []
        for c in range(3):
            old = around(x, c)
            viscous = jnp.zeros((ey, depth), jnp.float32)
            for n in range(6):
                viscous = viscous + faces[n] * (old[n + 1] - old[0])
            slope = pressure[1 + 2 * c] - pressure[0]
            force = total[half, xi, c]
            low0 = rims[0, half, xi, 3 * c : 3 * c + 1, :]
            low1 = rims[0, half, xi, 3 * c + 1 : 3 * c + 2, :]
            top = rims[1, half, xi, 3 * c + 2 : 3 * c + 3, :]
            force = force + jnp.where(
                row == 0, low0, jnp.where(row == 1, low1, jnp.where(row == ey - 1, top, 0.0))
            )
            new = old[0] + 0.5 * (viscous - slope + force)
            fresh_ref[x, c] = new
            field_ref[here + x, c] = new.astype(jnp.bfloat16)
            edge_rows += [new[0:2], new[ey - 1 : ey]]
        edge_rows.append(jnp.zeros((ey - 9, depth), jnp.float32))
        my_rim[x] = jnp.concatenate(edge_rows, axis=0).astype(jnp.bfloat16)
        if i == hx - 1:
            lax.fori_loop(1, slabs, start_field, 0)

    near_copies = (
        (has_high, has_low, copy(my_rim, near_rim.at[0], sem_near, (0,), (f, s + 1, t)), 0),
        (has_low, has_high, copy(my_rim, near_rim.at[1], sem_near, (1,), (f, s - 1, t)), 1),
    )
    for sends, receives, item, slot in near_copies:
        pl.when(sends)(item.start)

        @pl.when(jnp.logical_not(receives))
        def _(slot=slot):
            near_rim[slot] = jnp.zeros(near_rim.shape[1:], near_rim.dtype)

    def edge_copy(slab, d, to):
        part = field_ref.at[pl.ds(1 + ex * slab + hx * t, hx), 3]
        return copy(part, part, sem_edge, (d,), (to, s, t))

    def forward_copy(slab, d, core):
        part = field_ref.at[pl.ds(1 + ex * slab + hx * core, hx)]
        return copy(part, part, sem_forward, (d,), other)

    for outside in (0, slabs * ex + 1, slabs * ex + 2):
        field_ref[outside] = jnp.zeros(field_ref.shape[1:], field_ref.dtype)
    for sends, receives, item, slot in near_copies:
        pl.when(receives)(item.wait_recv)
    rim_turn = lax.rem(row, 3)
    for x in range(ex):
        field_ref[here + x, 3] = jnp.where(
            rim_turn == 2,
            near_rim[0, x].astype(jnp.float32),
            near_rim[1, x].astype(jnp.float32),
        ).astype(jnp.bfloat16)

    def start_edge(d, carry):
        edge_copy(f, d, lax.rem(f + d, slabs)).start()
        return carry

    lax.fori_loop(1, slabs, start_edge, 0)

    def forward(d, carry):
        slab = lax.rem(f + slabs - d, slabs)
        field_copy(slab, d, f).wait_recv()
        edge_copy(slab, d, f).wait_recv()
        forward_copy(slab, d, t).start()
        return carry

    lax.fori_loop(1, slabs, forward, 0)

    def finish(d, carry):
        slab = lax.rem(f + slabs - d, slabs)
        forward_copy(slab, d, 1 - t).wait_recv()
        forward_copy(slab, d, t).wait_send()
        field_copy(f, d, lax.rem(f + d, slabs)).wait_send()
        edge_copy(f, d, lax.rem(f + d, slabs)).wait_send()
        slab_copy(d).wait_send()
        return carry

    lax.fori_loop(1, slabs, finish, 0)

    def sent_pair(d, carry):
        pair_copy(d).wait_send()
        return carry

    lax.fori_loop(0, slabs, sent_pair, 0)
    total_copy.wait_send()
    for item in x_copies + y_copies + near_copies:
        pl.when(item[0])(item[2].wait_send)
    for sends, slot in ((has_high, 0), (has_low, 1)):

        @pl.when(sends)
        def _(slot=slot):
            for core in range(2):
                pltpu.make_async_remote_copy(
                    src_ref=total.at[t, :, 3],
                    dst_ref=rims.at[slot, t],
                    send_sem=sem_rim.at[0, slot, core],
                    recv_sem=sem_rim.at[1, slot, t],
                    device_id=other,
                    device_id_type=MESH,
                ).wait_send()


def body(slabs, subs, velocity, pressure, viscosity, marker_force, marker_offset, cell_base,
         block_slab):
    ex, ey, _, depth = velocity.shape
    hx = ex // 2
    blocks, _, markers = marker_force.shape
    width = slabs * ex + REACH
    bf16, f32 = jnp.bfloat16, jnp.float32
    vmem = pl.BlockSpec(memory_space=pltpu.VMEM)
    smem = pl.BlockSpec(memory_space=pltpu.SMEM)
    tile = ey * depth
    field_bytes = width * 4 * tile * 2
    target = block_slab[:, 0]
    forces, offsets, bases = (
        jnp.transpose(a, (1, 0, 2)) for a in (marker_force, marker_offset, cell_base)
    )

    parts = pl.pallas_call(
        functools.partial(spread_kernel, ex, ey),
        out_shape=jax.ShapeDtypeStruct((slabs * ex, 4, ey, depth), bf16),
        in_specs=[smem, vmem, vmem, vmem],
        out_specs=vmem,
        scratch_shapes=[
            pltpu.VMEM((width, 3, ey + RIM, depth), f32),
            pltpu.VMEM((2, 4, blocks, markers), f32),
            pltpu.VMEM((3, 4, blocks, markers), f32),
        ],
        compiler_params=pltpu.CompilerParams(
            vmem_limit_bytes=width * 3 * (ey + RIM) * depth * 4 + field_bytes + 12 * MIB
        ),
        name="spread",
    )(target, forces, offsets, bases)

    dma = pltpu.SemaphoreType.DMA
    half = (hx, 4, ey, depth)
    fresh, field = pl.pallas_call(
        functools.partial(grid_kernel, slabs, subs),
        out_shape=(
            jax.ShapeDtypeStruct((ex, 3, ey, depth), f32),
            jax.ShapeDtypeStruct((width, 4, ey, depth), bf16),
        ),
        in_specs=[vmem, vmem, vmem, vmem],
        out_specs=(vmem, vmem),
        scratch_shapes=[
            pltpu.VMEM((ex + 2, 5, ey, depth), f32),
            pltpu.VMEM((slabs,) + half, bf16),
            pltpu.VMEM((slabs,) + half, bf16),
            pltpu.VMEM((slabs,) + half, bf16),
            pltpu.VMEM((2,) + half, f32),
            pltpu.VMEM((2, 2, hx, ey, depth), f32),
            pltpu.VMEM((2, ex, 5, 8, depth), f32),
            pltpu.VMEM((ex, ey, depth), bf16),
            pltpu.VMEM((2, ex, ey, depth), bf16),
            dma((2, slabs)),
            dma((2, slabs)),
            dma((2, 2)),
            dma((2, 2, 2)),
            dma((2, 2)),
            dma((2, 2)),
            dma((2, 2)),
            dma((2, slabs)),
            dma((2, slabs)),
            dma((2, slabs)),
        ],
        compiler_params=pltpu.CompilerParams(
            collective_id=0,
            has_side_effects=True,
            vmem_limit_bytes=4 * field_bytes + 12 * MIB,
        ),
        name="grid",
    )(jnp.transpose(velocity, (0, 2, 1, 3)), pressure, viscosity, parts.reshape((slabs, 2) + half))

    marker_velocity, fresh = pl.pallas_call(
        functools.partial(sample_kernel, ex, ey),
        out_shape=(
            jax.ShapeDtypeStruct((3, blocks, markers), f32),
            jax.ShapeDtypeStruct(fresh.shape, f32),
        ),
        in_specs=[smem, vmem, vmem, vmem, vmem],
        out_specs=(vmem, vmem),
        scratch_shapes=[pltpu.VMEM((3, 4, blocks, markers), f32)],
        compiler_params=pltpu.CompilerParams(vmem_limit_bytes=field_bytes + 12 * MIB),
        name="sample",
    )(target, offsets, bases, field, fresh)
    return (jnp.transpose(fresh, (0, 2, 1, 3)), jnp.transpose(marker_velocity, (1, 0, 2)))


def solution(mesh):
    marker = P(("fluid", "sub", "struct"), None, None)
    return jax.shard_map(
        functools.partial(body, mesh.shape["fluid"], mesh.shape["sub"]),
        mesh=mesh,
        in_specs=(
            P("fluid", "sub", None, None),
            P("fluid", "sub", None),
            P("fluid", "sub", None),
            marker,
            marker,
            marker,
            P(("fluid", "sub", "struct"), None),
        ),
        out_specs=(P("fluid", "sub", None, None), marker),
        check_vma=False,
    )
```

```python
import functools

import jax
import jax.numpy as jnp
from jax import lax
from jax.experimental import pallas as pl
from jax.experimental.pallas import tpu as pltpu
from jax.sharding import PartitionSpec as P

MESH = pl.DeviceIdType.MESH
RIM = 8
REACH = 3
MIB = 1 << 20
UNROLL = 8


def stencil(offsets):
    root = jnp.sqrt(1.0 + 4.0 * offsets - 4.0 * offsets * offsets)
    low = 3.0 - 2.0 * offsets
    high = 1.0 + 2.0 * offsets
    return (
        (low - root) * 0.125,
        (low + root) * 0.125,
        (high + root) * 0.125,
        (high - root) * 0.125,
    )


def place(weights, shift):
    result = jnp.zeros(shift.shape, jnp.float32)
    for n in range(4):
        result = jnp.where(shift == n - 1, weights[n], result)
    return result


def at_cells(base, depth, markers):
    cells = lax.broadcasted_iota(jnp.int32, (depth, markers), 0).astype(jnp.int16)
    shift = cells - jnp.broadcast_to(base, (16, markers)).astype(jnp.int16)[0:1]
    return [shift == jnp.int16(n - 1) for n in range(4)]


def choose(where, values):
    result = jnp.zeros(where[0].shape, jnp.bfloat16)
    for mask, value in zip(where, values):
        value = jnp.broadcast_to(value, (16, value.shape[1])).astype(jnp.bfloat16)[0:1]
        result = jnp.where(mask, value, result)
    return result


def spread_kernel(ex, ey, slab_ref, force_ref, offset_ref, base_ref, out_ref, acc, held, loads):
    _, blocks, markers = force_ref.shape
    depth = acc.shape[3]
    rows = ey + RIM
    span = ex + REACH
    acc[...] = jnp.zeros_like(acc)
    for axis in range(3):
        for n, weight in enumerate(stencil(offset_ref[axis])):
            if axis < 2:
                held[axis, n] = weight
            else:
                for c in range(3):
                    loads[c, n] = force_ref[c] * weight
    xs = lax.broadcasted_iota(jnp.int32, (span, markers), 0) - 1
    ys = lax.broadcasted_iota(jnp.int32, (rows, markers), 0)
    ys = jnp.where(ys == ey + 2, -1, jnp.where(ys > ey + 2, -100, ys))

    def step(b, carry):
        start = slab_ref[b] * ex
        one = pl.ds(b, 1)
        wx = place([held[0, n, one] for n in range(4)], xs - base_ref[0, one])
        wy = place([held[1, n, one] for n in range(4)], ys - base_ref[1, one])
        where = at_cells(base_ref[2, one], depth, markers)
        plane = jnp.concatenate([wx[i : i + 1] * wy for i in range(span)], axis=0)
        plane = plane.astype(jnp.bfloat16)
        for c in range(3):
            loaded = choose(where, [loads[c, n, one] for n in range(4)])
            term = lax.dot_general(
                plane, loaded, (((1,), (1,)), ((), ())), preferred_element_type=jnp.float32
            )
            acc[pl.ds(start, span), c] += term.reshape(span, rows, depth)
        return carry

    lax.fori_loop(0, blocks, step, 0, unroll=UNROLL)

    def pack(x, carry):
        for c in range(3):
            out_ref[x, c] = acc[x + 1, c, 0:ey, :].astype(jnp.bfloat16)
        parts = [acc[x + 1, c, ey : ey + 3, :] for c in range(3)]
        parts.append(jnp.zeros((ey - 9, depth), jnp.float32))
        out_ref[x, 3] = jnp.concatenate(parts, axis=0).astype(jnp.bfloat16)
        return carry

    lax.fori_loop(0, out_ref.shape[0], pack, 0)


def sample_kernel(
    ex, ey, slab_ref, offset_ref, base_ref, field_ref, new_ref, out_ref, fresh_ref, held
):
    _, blocks, markers = offset_ref.shape
    depth = field_ref.shape[3]
    span = ex + REACH
    fresh_ref[...] = new_ref[...]
    for axis in range(3):
        for n, weight in enumerate(stencil(offset_ref[axis])):
            held[axis, n] = weight
    xs = lax.broadcasted_iota(jnp.int32, (span, markers), 0) - 1
    ys = lax.broadcasted_iota(jnp.int32, (ey, markers), 0)
    turn = ys % 3
    rim = jnp.where(ys >= 9, -100, jnp.where(turn == 2, -1, ey + turn))

    def step(b, carry):
        start = slab_ref[b] * ex
        one = pl.ds(b, 1)
        weights = [[held[axis, n, one] for n in range(4)] for axis in range(3)]
        wx = place(weights[0], xs - base_ref[0, one])
        wy = place(weights[1], ys - base_ref[1, one])
        wr = place(weights[1], rim - base_ref[1, one])
        where = at_cells(base_ref[2, one], depth, markers)
        wz = choose(where, weights[2])
        cells = field_ref[pl.ds(start, span)].reshape(span * 4 * ey, depth)
        sums = jnp.dot(cells, wz, preferred_element_type=jnp.float32)
        sums = sums.reshape(span, 4 * ey, markers)
        across = sums[0] * wx[0:1]
        for i in range(1, span):
            across = across + sums[i] * wx[i : i + 1]
        edge = across[3 * ey : 4 * ey] * wr
        for c in range(3):
            own = jnp.sum(across[c * ey : (c + 1) * ey] * wy, axis=0, keepdims=True)
            beside = jnp.sum(edge[3 * c : 3 * c + 3], axis=0, keepdims=True)
            out_ref[c, one] = own + beside
        return carry

    lax.fori_loop(0, blocks, step, 0, unroll=UNROLL)


def grid_kernel(
    slabs, subs,
    velocity_ref, pressure_ref, viscosity_ref, part_ref, fresh_ref, field_ref,
    old_ref, pair, outgoing, incoming, total, rims, yhalo, my_rim, near_rim,
    sem_pair, sem_slab, sem_total, sem_rim, sem_x, sem_y, sem_near,
    sem_field, sem_edge, sem_forward, sem_stage,
):
    f, s, t = lax.axis_index("fluid"), lax.axis_index("sub"), lax.axis_index("struct")
    ex, _, ey, depth = velocity_ref.shape
    hx = ex // 2
    other = (f, s, 1 - t)
    has_low, has_high = s > 0, s < subs - 1
    has_left, has_right = f > 0, f < slabs - 1

    def copy(src, dst, sems, index, device):
        return pltpu.make_async_remote_copy(
            src_ref=src,
            dst_ref=dst,
            send_sem=sems.at[(0,) + index],
            recv_sem=sems.at[(1,) + index],
            device_id=device,
            device_id_type=MESH,
        )

    stages = (
        pltpu.make_async_copy(velocity_ref, old_ref.at[1 : ex + 1, 0:3], sem_stage.at[0]),
        pltpu.make_async_copy(pressure_ref, old_ref.at[1 : ex + 1, 3], sem_stage.at[1]),
        pltpu.make_async_copy(viscosity_ref, old_ref.at[1 : ex + 1, 4], sem_stage.at[2]),
    )
    for item in stages:
        item.start()

    barrier = pltpu.get_barrier_semaphore()

    def greet(device):
        pl.semaphore_signal(barrier, inc=1, device_id=device, device_id_type=MESH)

    greet(other)

    def greet_slab(d, carry):
        greet((lax.rem(f + d, slabs), s, t))
        return carry

    lax.fori_loop(1, slabs, greet_slab, 0)
    for present, step in ((has_low, -1), (has_high, 1)):

        @pl.when(present)
        def _(step=step):
            greet((f, s + step, t))
            greet((f, s + step, 1 - t))

    beside = has_low.astype(jnp.int32) + has_high.astype(jnp.int32)
    pl.semaphore_wait(barrier, slabs + 2 * beside)

    def pair_copy(slab):
        return copy(part_ref.at[slab, 1 - t], pair.at[slab], sem_pair, (slab,), other)

    def start_pair(d, carry):
        pair_copy(lax.rem(f + d, slabs)).start()
        return carry

    lax.fori_loop(1, slabs + 1, start_pair, 0)

    for item in stages:
        item.wait()
    x_copies = (
        (has_left, has_right,
         copy(old_ref.at[1], old_ref.at[ex + 1], sem_x, (1,), (f - 1, s, t)), old_ref, ex + 1),
        (has_right, has_left,
         copy(old_ref.at[ex], old_ref.at[0], sem_x, (0,), (f + 1, s, t)), old_ref, 0),
    )
    y_copies = (
        (has_low, has_high,
         copy(old_ref.at[1 : ex + 1, :, 0:8], yhalo.at[1], sem_y, (1,), (f, s - 1, t)), yhalo, 1),
        (has_high, has_low,
         copy(old_ref.at[1 : ex + 1, :, ey - 8 : ey], yhalo.at[0], sem_y, (0,), (f, s + 1, t)),
         yhalo, 0),
    )
    for sends, receives, item, halo, slot in x_copies + y_copies:
        pl.when(sends)(item.start)

        @pl.when(jnp.logical_not(receives))
        def _(halo=halo, slot=slot):
            halo[slot] = jnp.zeros(halo.shape[1:], halo.dtype)

    def slab_copy(d):
        return copy(
            outgoing.at[d], incoming.at[d], sem_slab, (d,), (lax.rem(f + d, slabs), s, t)
        )

    def send_slab(d, carry):
        slab = lax.rem(f + d, slabs)
        pair_copy(slab).wait_recv()
        both = part_ref[slab, t].astype(jnp.float32) + pair[slab].astype(jnp.float32)
        outgoing[d] = both.astype(jnp.bfloat16)
        slab_copy(d).start()
        return carry

    lax.fori_loop(1, slabs, send_slab, 0)
    pair_copy(f).wait_recv()
    total[t] = part_ref[f, t].astype(jnp.float32) + pair[f].astype(jnp.float32)

    def add_slab(d, carry):
        slab_copy(d).wait_recv()
        total[t] += incoming[d].astype(jnp.float32)
        return carry

    lax.fori_loop(1, slabs, add_slab, 0)

    total_copy = copy(total.at[t], total.at[t], sem_total, (t,), other)
    total_back = copy(total.at[1 - t], total.at[1 - t], sem_total, (1 - t,), other)
    total_copy.start()
    for sends, receives, step, slot in ((has_high, has_low, 1, 0), (has_low, has_high, -1, 1)):

        @pl.when(sends)
        def _(step=step, slot=slot):
            for core in range(2):
                to = lax.rem(t + core, 2)
                pltpu.make_async_remote_copy(
                    src_ref=total.at[t, :, 3],
                    dst_ref=rims.at[slot, t],
                    send_sem=sem_rim.at[0, slot, core],
                    recv_sem=sem_rim.at[1, slot, t],
                    device_id=(f, s + step, to),
                    device_id_type=MESH,
                ).start()

        @pl.when(jnp.logical_not(receives))
        def _(slot=slot):
            rims[slot] = jnp.zeros(rims.shape[1:], rims.dtype)

    for _, receives, item, _, _ in x_copies + y_copies:
        pl.when(receives)(item.wait_recv)
    total_back.wait_recv()
    for receives, slot in ((has_low, 0), (has_high, 1)):

        @pl.when(receives)
        def _(slot=slot):
            for core in range(2):
                pltpu.make_async_remote_copy(
                    src_ref=total.at[t, :, 3],
                    dst_ref=rims.at[slot, core],
                    send_sem=sem_rim.at[0, slot, core],
                    recv_sem=sem_rim.at[1, slot, core],
                    device_id=other,
                    device_id_type=MESH,
                ).wait_recv()

    row = lax.broadcasted_iota(jnp.int32, (ey, depth), 0)
    lane = lax.broadcasted_iota(jnp.int32, (ey, depth), 1)
    here = 1 + ex * f

    def around(x, i):
        mid = old_ref[x + 1, i]
        return (
            mid,
            old_ref[x + 2, i],
            old_ref[x, i],
            jnp.where(row == ey - 1, yhalo[1, x, i, 0:1, :], pltpu.roll(mid, ey - 1, 0)),
            jnp.where(row == 0, yhalo[0, x, i, 7:8, :], pltpu.roll(mid, 1, 0)),
            jnp.where(lane == depth - 1, 0.0, pltpu.roll(mid, depth - 1, 1)),
            jnp.where(lane == 0, 0.0, pltpu.roll(mid, 1, 1)),
        )

    def field_copy(slab, d, to):
        part = field_ref.at[pl.ds(1 + ex * slab + hx * t, hx), 0:3]
        return copy(part, part, sem_field, (d,), (to, s, t))

    def start_field(d, carry):
        field_copy(f, d, lax.rem(f + d, slabs)).start()
        return carry

    for i in range(ex):
        x = lax.rem(hx * t + i, ex)
        pressure = around(x, 3)
        viscosity = around(x, 4)
        faces = [0.5 * (viscosity[0] + beside) for beside in viscosity[1:]]
        half, xi = (t, i) if i < hx else (1 - t, i - hx)
        edge_rows = []
        for c in range(3):
            old = around(x, c)
            viscous = jnp.zeros((ey, depth), jnp.float32)
            for n in range(6):
                viscous = viscous + faces[n] * (old[n + 1] - old[0])
            slope = pressure[1 + 2 * c] - pressure[0]
            force = total[half, xi, c]
            low0 = rims[0, half, xi, 3 * c : 3 * c + 1, :]
            low1 = rims[0, half, xi, 3 * c + 1 : 3 * c + 2, :]
            top = rims[1, half, xi, 3 * c + 2 : 3 * c + 3, :]
            force = force + jnp.where(
                row == 0, low0, jnp.where(row == 1, low1, jnp.where(row == ey - 1, top, 0.0))
            )
            new = old[0] + 0.5 * (viscous - slope + force)
            fresh_ref[x, c] = new
            field_ref[here + x, c] = new.astype(jnp.bfloat16)
            edge_rows += [new[0:2], new[ey - 1 : ey]]
        edge_rows.append(jnp.zeros((ey - 9, depth), jnp.float32))
        my_rim[x] = jnp.concatenate(edge_rows, axis=0).astype(jnp.bfloat16)
        if i == hx - 1:
            lax.fori_loop(1, slabs, start_field, 0)

    near_copies = (
        (has_high, has_low, copy(my_rim, near_rim.at[0], sem_near, (0,), (f, s + 1, t)), 0),
        (has_low, has_high, copy(my_rim, near_rim.at[1], sem_near, (1,), (f, s - 1, t)), 1),
    )
    for sends, receives, item, slot in near_copies:
        pl.when(sends)(item.start)

        @pl.when(jnp.logical_not(receives))
        def _(slot=slot):
            near_rim[slot] = jnp.zeros(near_rim.shape[1:], near_rim.dtype)

    def edge_copy(slab, d, to):
        part = field_ref.at[pl.ds(1 + ex * slab + hx * t, hx), 3]
        return copy(part, part, sem_edge, (d,), (to, s, t))

    def forward_copy(slab, d, core):
        part = field_ref.at[pl.ds(1 + ex * slab + hx * core, hx)]
        return copy(part, part, sem_forward, (d,), other)

    for outside in (0, slabs * ex + 1, slabs * ex + 2):
        field_ref[outside] = jnp.zeros(field_ref.shape[1:], field_ref.dtype)
    for sends, receives, item, slot in near_copies:
        pl.when(receives)(item.wait_recv)
    rim_turn = lax.rem(row, 3)
    for x in range(ex):
        field_ref[here + x, 3] = jnp.where(
            rim_turn == 2,
            near_rim[0, x].astype(jnp.float32),
            near_rim[1, x].astype(jnp.float32),
        ).astype(jnp.bfloat16)

    def start_edge(d, carry):
        edge_copy(f, d, lax.rem(f + d, slabs)).start()
        return carry

    lax.fori_loop(1, slabs, start_edge, 0)

    def forward(d, carry):
        slab = lax.rem(f + slabs - d, slabs)
        field_copy(slab, d, f).wait_recv()
        edge_copy(slab, d, f).wait_recv()
        forward_copy(slab, d, t).start()
        return carry

    lax.fori_loop(1, slabs, forward, 0)

    def finish(d, carry):
        slab = lax.rem(f + slabs - d, slabs)
        forward_copy(slab, d, 1 - t).wait_recv()
        forward_copy(slab, d, t).wait_send()
        field_copy(f, d, lax.rem(f + d, slabs)).wait_send()
        edge_copy(f, d, lax.rem(f + d, slabs)).wait_send()
        slab_copy(d).wait_send()
        return carry

    lax.fori_loop(1, slabs, finish, 0)

    def sent_pair(d, carry):
        pair_copy(d).wait_send()
        return carry

    lax.fori_loop(0, slabs, sent_pair, 0)
    total_copy.wait_send()
    for item in x_copies + y_copies + near_copies:
        pl.when(item[0])(item[2].wait_send)
    for sends, slot in ((has_high, 0), (has_low, 1)):

        @pl.when(sends)
        def _(slot=slot):
            for core in range(2):
                pltpu.make_async_remote_copy(
                    src_ref=total.at[t, :, 3],
                    dst_ref=rims.at[slot, t],
                    send_sem=sem_rim.at[0, slot, core],
                    recv_sem=sem_rim.at[1, slot, t],
                    device_id=other,
                    device_id_type=MESH,
                ).wait_send()


def body(slabs, subs, velocity, pressure, viscosity, marker_force, marker_offset, cell_base,
         block_slab):
    ex, ey, _, depth = velocity.shape
    hx = ex // 2
    blocks, _, markers = marker_force.shape
    width = slabs * ex + REACH
    bf16, f32 = jnp.bfloat16, jnp.float32
    vmem = pl.BlockSpec(memory_space=pltpu.VMEM)
    anywhere = pl.BlockSpec(memory_space=pl.ANY)
    smem = pl.BlockSpec(memory_space=pltpu.SMEM)
    tile = ey * depth
    field_bytes = width * 4 * tile * 2
    target = block_slab[:, 0]
    forces, offsets, bases = (
        jnp.transpose(a, (1, 0, 2)) for a in (marker_force, marker_offset, cell_base)
    )

    parts = pl.pallas_call(
        functools.partial(spread_kernel, ex, ey),
        out_shape=jax.ShapeDtypeStruct((slabs * ex, 4, ey, depth), bf16),
        in_specs=[smem, vmem, vmem, vmem],
        out_specs=vmem,
        scratch_shapes=[
            pltpu.VMEM((width, 3, ey + RIM, depth), f32),
            pltpu.VMEM((2, 4, blocks, markers), f32),
            pltpu.VMEM((3, 4, blocks, markers), f32),
        ],
        compiler_params=pltpu.CompilerParams(
            vmem_limit_bytes=56 * MIB
        ),
        name="spread",
    )(target, forces, offsets, bases)

    dma = pltpu.SemaphoreType.DMA
    half = (hx, 4, ey, depth)
    fresh, field = pl.pallas_call(
        functools.partial(grid_kernel, slabs, subs),
        out_shape=(
            jax.ShapeDtypeStruct((ex, 3, ey, depth), f32),
            jax.ShapeDtypeStruct((width, 4, ey, depth), bf16),
        ),
        in_specs=[anywhere, anywhere, anywhere, vmem],
        out_specs=(vmem, vmem),
        scratch_shapes=[
            pltpu.VMEM((ex + 2, 5, ey, depth), f32),
            pltpu.VMEM((slabs,) + half, bf16),
            pltpu.VMEM((slabs,) + half, bf16),
            pltpu.VMEM((slabs,) + half, bf16),
            pltpu.VMEM((2,) + half, f32),
            pltpu.VMEM((2, 2, hx, ey, depth), f32),
            pltpu.VMEM((2, ex, 5, 8, depth), f32),
            pltpu.VMEM((ex, ey, depth), bf16),
            pltpu.VMEM((2, ex, ey, depth), bf16),
            dma((2, slabs)),
            dma((2, slabs)),
            dma((2, 2)),
            dma((2, 2, 2)),
            dma((2, 2)),
            dma((2, 2)),
            dma((2, 2)),
            dma((2, slabs)),
            dma((2, slabs)),
            dma((2, slabs)),
            dma((3,)),
        ],
        compiler_params=pltpu.CompilerParams(
            collective_id=0,
            has_side_effects=True,
            vmem_limit_bytes=max(4 * field_bytes + 12 * MIB, 48 * MIB),
        ),
        name="grid",
    )(jnp.transpose(velocity, (0, 2, 1, 3)), pressure, viscosity, parts.reshape((slabs, 2) + half))

    marker_velocity, fresh = pl.pallas_call(
        functools.partial(sample_kernel, ex, ey),
        out_shape=(
            jax.ShapeDtypeStruct((3, blocks, markers), f32),
            jax.ShapeDtypeStruct(fresh.shape, f32),
        ),
        in_specs=[smem, vmem, vmem, vmem, vmem],
        out_specs=(vmem, vmem),
        scratch_shapes=[pltpu.VMEM((3, 4, blocks, markers), f32)],
        compiler_params=pltpu.CompilerParams(vmem_limit_bytes=field_bytes + 12 * MIB),
        name="sample",
    )(target, offsets, bases, field, fresh)
    return (jnp.transpose(fresh, (0, 2, 1, 3)), jnp.transpose(marker_velocity, (1, 0, 2)))


def solution(mesh):
    marker = P(("fluid", "sub", "struct"), None, None)
    return jax.shard_map(
        functools.partial(body, mesh.shape["fluid"], mesh.shape["sub"]),
        mesh=mesh,
        in_specs=(
            P("fluid", "sub", None, None),
            P("fluid", "sub", None),
            P("fluid", "sub", None),
            marker,
            marker,
            marker,
            P(("fluid", "sub", "struct"), None),
        ),
        out_specs=(P("fluid", "sub", None, None), marker),
        check_vma=False,
    )
```
